1024 devices in a mesh: section: 16 (over y, x_hi), expert: 32 (over z, core), dp: 2 (over x_lo).
Axes of the slice: x: 4 (x_hi: 2, x_lo: 2; x = x_hi * 2 + x_lo), y: 8, z: 16, core: 2. Of those that a mesh axis runs over, the one named last changes fastest.
Arguments:
- grad_in: bfloat16 [2, 16, 4096, 3584], P(None, 'section', ('expert', 'dp')), may hold values from -6 to 6
- expert_ids: int32 [2, 16, 4096, 1], P(None, 'section', ('expert', 'dp')), may hold values from 0 to 31; in each aligned block of 64 rows (0 to 63, 64 to 127, ..., all dimensions but the last counted through in order) at most 3 rows name the same one
- gate_weights: float32 [16, 4096], P('section', ('expert', 'dp')), may hold values from 0.2 to 1
- back_rows: bfloat16 [16, 2, 32, 96, 3584], P('section', 'dp', 'expert'), may hold values from -6 to 6
- shared_down: bfloat16 [16, 1024, 3584], P('section', 'dp'), may hold values from -0.09375 to 0.09375
Outputs:
- dispatch_rows: bfloat16 [16, 2, 32, 96, 3584], P('section', 'dp', 'expert')
- section_grad: bfloat16 [16, 4096, 3584], P('section', ('expert', 'dp'))
- shared_grad: bfloat16 [2, 16, 4096, 1024], P(None, 'section', 'expert', 'dp')
The draws below stay inside these ranges and needn't reach their ends.
Inputs may be any that keep to these rules, and one draw needn't show every extreme that they name: `expert_ids`: within the 64 tokens of one device block of one micro-batch and section, at most 3 tokens name the same expert, a bound that some block reaches.
All inputs are finite; a program needn't handle non-finite values.
Results may differ from the reference program's by a relative error of at most 0.001.
Values may be sent and summed in bfloat16 or wider, within the bound.
No kernel may reach another device: no remote copies, remote signals or barrier semaphores. Data moves between devices by JAX's collectives and lax.ppermute only.
A program may use at most 64 MiB of HBM per device.

```python
import math
import jax
import jax.numpy as jnp
import numpy as np
from jax import lax

D = 3584
FF = 1024
TOK_DEV = 64
EXPERTS = 32
CAP = 3
TOKENS = 4096
N_SECTION = 16
N_EXPERT = 32
N_DP = 2


def block_scale(stream_key, dims, split, least, high):
    level = 1.0
    for position, blocks in split:
        steps = jax.random.uniform(jax.random.fold_in(jax.random.fold_in(stream_key, 6), position), (blocks,), jnp.float32, least / len(split), high / len(split))
        level = level * jnp.repeat(jnp.exp(steps), dims[position] // blocks).reshape((-1,) + (1,) * (len(dims) - 1 - position))
    return level


def deal_out(own_key, own, number, rows, amount, top, reach, lean):
    sequence = jax.random.permutation(own_key, amount)
    crowded, ordinary = load_shares(amount, rows * top, reach, lean, True), load_shares(amount, rows * top, reach, lean, False)
    places = jnp.arange(amount)

    def named(tallies, rotation):
        used = int((tallies > 0).sum())
        fixed = max(1, used // 4)
        shifted = fixed + (places - fixed + rotation * (used - fixed)) % max(1, amount - fixed)
        return jnp.zeros((amount,), jnp.int32).at[sequence[jnp.where(places < fixed, places, shifted)]].set(jnp.asarray(tallies, jnp.int32))

    tallies = jnp.where(number % 4 == 0, named(crowded, number // 4), named(ordinary, number - number // 4 - 1))
    mixed = jax.random.permutation(jax.random.fold_in(own, 3), amount)
    source_of, sink = mixed[0:amount // 2 * 2:2], mixed[1:amount // 2 * 2:2]
    slack = jnp.minimum(tallies[source_of] - 1, reach - tallies[sink]) // 2
    slack = jnp.where((source_of == sequence[0]) | (sink == sequence[0]) | (tallies[sink] == 0), 0, jnp.maximum(slack, 0))
    shifted = jax.random.randint(jax.random.fold_in(own, 4), (amount // 2,), 0, 1 << 20) % (slack + 1)
    tallies = tallies.at[source_of].add(-shifted).at[sink].add(shifted)
    items = jnp.searchsorted(jnp.cumsum(tallies), jnp.arange(rows * top), side="right").astype(jnp.int32)
    listing = items.reshape(top, rows).T
    listing = listing[jax.random.permutation(jax.random.fold_in(own, 1), rows)]
    rotation = jax.random.randint(jax.random.fold_in(own, 2), (rows, 1), 0, top)
    return jnp.take_along_axis(listing, (jnp.arange(top)[None, :] + rotation) % top, axis=1)


def load_shares(count, total, reach, lean, full):
    portions = [(1 << 20) // math.isqrt(standing ** lean) + 1 for standing in range(1, count + 1)]
    largest = reach if full else min(reach, max(-(-total // count), total * portions[0] // sum(portions)))
    least = 1 if total - largest >= count - 1 else 0
    counts, surplus = [largest] + [least] * (count - 1), total - largest - least * (count - 1)
    while surplus > 0:
        movable = [i for i in range(1, count) if counts[i] < largest] or [i for i in range(1, count) if counts[i] < reach]
        pool, remaining = sum([portions[i] for i in movable]), surplus
        for i in movable:
            extra = min(reach - counts[i], max(1, remaining * portions[i] // pool), surplus)
            counts[i] = counts[i] + extra
            surplus = surplus - extra
    return np.array(counts)


def gaussian(rng, extent, deviation, limit, shards=(), kind=jnp.bfloat16):
    values = jax.random.normal(rng, extent, jnp.float32) * deviation
    if len(shards) > 0:
        values = block_scale(rng, extent, shards, -0.22, 0.18) * values
    return jnp.clip(values, min=-limit, max=limit).astype(kind)


def setup_inputs(seed: int = 0) -> dict:
    key_of = jax.random.split(jax.random.key(seed), 6)
    grad_in = gaussian(key_of[0], (2, N_SECTION, TOKENS, D), 1.0, 6.0, ((1, 16), (2, 64)))
    expert_ids_keys = jax.random.split(jax.random.fold_in(key_of[1], 1), 2 * N_SECTION * TOKENS // TOK_DEV)
    expert_ids_turns = jax.random.permutation(jax.random.fold_in(key_of[1], 3), 2 * N_SECTION * TOKENS // TOK_DEV)
    expert_ids = jax.vmap(lambda own, number: deal_out(jax.random.fold_in(key_of[1], 2), own, number, TOK_DEV, EXPERTS, 1, CAP, 2))(expert_ids_keys, expert_ids_turns).reshape((2, N_SECTION, TOKENS, 1))
    gate_weights = jnp.clip(0.2 + 0.8 * jax.random.uniform(key_of[2], (N_SECTION, TOKENS), jnp.float32) ** block_scale(key_of[2], (N_SECTION, TOKENS), ((0, 16), (1, 64)), -0.2, 0.2), 0.2, 1.0)
    back_rows = gaussian(key_of[3], (N_SECTION, N_DP, EXPERTS, N_EXPERT * CAP, D), 1.0, 6.0, ((0, 16), (1, 2), (2, 32)))
    shared_down = gaussian(key_of[4], (N_SECTION, FF, D), D ** -0.5, 0.09375, ((0, 16), (1, 2)))
    return dict(grad_in=grad_in, expert_ids=expert_ids, gate_weights=gate_weights, back_rows=back_rows, shared_down=shared_down)


def block_slots(ident):
    blocks = ident.reshape(-1, TOK_DEV)
    onehot = (blocks[:, :, None] == jnp.arange(EXPERTS, dtype=jnp.int32)[None, None, :]).astype(jnp.int32)
    earlier = jnp.cumsum(onehot, axis=1) - onehot
    return jnp.sum(earlier * onehot, axis=2).reshape(-1).astype(jnp.int32)


def one_section(operands):
    from_next, from_prev, ident_a, ident_b, weight_row, returning, down_part = operands
    token_pos = jnp.arange(TOKENS, dtype=jnp.int32)
    block_id = token_pos // TOK_DEV
    source_expert = block_id // N_DP
    replica = block_id % N_DP
    slot_a = block_slots(ident_a)
    scaled = (weight_row[:, None] * from_next.astype(jnp.float32)).astype(jnp.bfloat16)
    dispatched = jnp.zeros((N_DP, EXPERTS, N_EXPERT * CAP, D), jnp.bfloat16)
    dispatched = dispatched.at[replica, ident_a, source_expert * CAP + slot_a].set(scaled)
    slot_b = block_slots(ident_b)
    picked = returning[replica, ident_b, source_expert * CAP + slot_b]
    section_grad = (from_prev.astype(jnp.float32) + picked.astype(jnp.float32)).astype(jnp.bfloat16)
    hidden_a = jnp.dot(from_next, down_part.T, preferred_element_type=jnp.float32).astype(jnp.bfloat16)
    hidden_b = jnp.dot(from_prev, down_part.T, preferred_element_type=jnp.float32).astype(jnp.bfloat16)
    return dispatched, section_grad, jnp.stack([hidden_a, hidden_b])


def reference(grad_in, expert_ids, gate_weights, back_rows, shared_down):
    zeros_block = jnp.zeros_like(grad_in[0, :1])
    from_next = jnp.concatenate([grad_in[0, 1:], zeros_block], axis=0)
    from_prev = jnp.concatenate([zeros_block, grad_in[1, :-1]], axis=0)
    dispatch_rows, section_grad, shared_grad = lax.map(one_section, (from_next, from_prev, expert_ids[0, :, :, 0], expert_ids[1, :, :, 0], gate_weights, back_rows, shared_down))
    return dispatch_rows, section_grad, jnp.transpose(shared_grad, (1, 0, 2, 3))
```

```python
import jax
import jax.numpy as jnp
from jax import lax
from jax.sharding import PartitionSpec as P

CORES = 2
PARTS = 4


def shifted(array, axis, by):
    peers = lax.axis_size(axis)
    pairs = [(i, i + by) for i in range(peers) if 0 <= i + by < peers]
    return lax.ppermute(array, axis, pairs)


def swapped(array, axis):
    peers = lax.axis_size(axis)
    return lax.ppermute(array, axis, [(i, i ^ 1) for i in range(peers)])


def slot_of(ident):
    same = ident[:, None] == ident[None, :]
    count = ident.shape[0]
    order = jnp.arange(count, dtype=jnp.int32)
    before = order[None, :] < order[:, None]
    return jnp.sum((same & before).astype(jnp.int32), axis=1)


def select(rows, width, dtype=jnp.bfloat16):
    return (rows[:, None] == jnp.arange(width, dtype=jnp.int32)[None, :]).astype(dtype)


def on_device(grad_in, expert_ids, gate_weights, back_rows, shared_down):
    hosts = lax.axis_size("expert")
    chips = hosts // CORES
    core = lax.axis_index("expert") % CORES
    other = 1 - core
    buffer_rows, width = back_rows.shape[3:]
    cap = buffer_rows // hosts
    chip_rows = CORES * cap
    part = width // PARTS
    across = [[CORES * z + c for z in range(chips)] for c in range(CORES)]

    def exchanged(pieces):
        return lax.all_to_all(
            pieces, "expert", split_axis=0, concat_axis=0, tiled=True, axis_index_groups=across
        )

    came = exchanged(back_rows[0, 0, 0].reshape(chips, chip_rows * PARTS, part))
    came = came.reshape(buffer_rows, width)

    from_next = shifted(grad_in[0, 0], "section", -1)
    from_prev = shifted(grad_in[1, 0], "section", 1)
    ident_a = expert_ids[0, 0, :, 0]
    ident_b = expert_ids[1, 0, :, 0]
    ident_mate = swapped(ident_a, "expert")

    scaled = (gate_weights[0][:, None] * from_next.astype(jnp.float32)).astype(jnp.bfloat16)
    scaled_mate = swapped(scaled, "expert")
    chip_tokens = jnp.concatenate([scaled, scaled_mate], axis=0)

    def place(ident, source):
        row = (ident // CORES) * chip_rows + source * cap + slot_of(ident)
        return jnp.where(ident % CORES == core, row, buffer_rows)

    target = jnp.concatenate([place(ident_a, core), place(ident_mate, other)])
    table = (jnp.arange(buffer_rows, dtype=jnp.int32)[:, None] == target[None, :]).astype(jnp.bfloat16)
    packed = jnp.dot(table, chip_tokens, preferred_element_type=jnp.float32).astype(jnp.bfloat16)
    sent = exchanged(packed.reshape(chips, chip_rows * PARTS, part)).reshape(buffer_rows, width)

    lines = jnp.arange(chips * cap, dtype=jnp.int32)
    passed = select((lines // cap) * chip_rows + other * cap + lines % cap, buffer_rows)
    passed = jnp.dot(passed, came, preferred_element_type=jnp.float32).astype(jnp.bfloat16)
    passed = swapped(passed, "expert")
    slot_b = slot_of(ident_b)
    here = ident_b % CORES == core
    from_own = jnp.where(here, (ident_b // CORES) * chip_rows + core * cap + slot_b, buffer_rows)
    from_mate = jnp.where(here, chips * cap, (ident_b // CORES) * cap + slot_b)
    returned = jnp.dot(
        select(from_own, buffer_rows), came, preferred_element_type=jnp.float32
    ) + jnp.dot(select(from_mate, chips * cap), passed, preferred_element_type=jnp.float32)
    section_grad = (from_prev.astype(jnp.float32) + returned).astype(jnp.bfloat16)

    replica = lax.axis_index("dp")
    down_part = shared_down[0]

    def hidden(own):
        mate = swapped(own, "dp")
        first = jnp.where(replica == 0, own, mate)
        second = jnp.where(replica == 0, mate, own)
        tokens = jnp.concatenate([first, second], axis=0)
        return jnp.einsum(
            "td,hd->th", tokens, down_part, preferred_element_type=jnp.float32
        ).astype(jnp.bfloat16)

    hidden_grad = jnp.stack([hidden(from_next), hidden(from_prev)])
    return (
        sent.reshape(1, 1, 1, buffer_rows, width),
        section_grad[None],
        hidden_grad[:, None],
    )


def solution(mesh):
    placed = (
        P(None, "section", ("expert", "dp"), None),
        P(None, "section", ("expert", "dp"), None),
        P("section", ("expert", "dp")),
        P("section", "dp", "expert", None, None),
        P("section", "dp", None),
    )
    return jax.shard_map(
        on_device,
        mesh=mesh,
        in_specs=placed,
        out_specs=(
            P("section", "dp", "expert", None, None),
            P("section", ("expert", "dp"), None),
            P(None, "section", "expert", "dp"),
        ),
        check_vma=False,
    )
```

```python
import jax
import jax.numpy as jnp
from jax import lax
from jax.sharding import PartitionSpec as P

CORES = 2
PARTS = 4


def shifted(array, axis, by):
    peers = lax.axis_size(axis)
    pairs = [(i, i + by) for i in range(peers) if 0 <= i + by < peers]
    return lax.ppermute(array, axis, pairs)


def swapped(array, axis):
    peers = lax.axis_size(axis)
    return lax.ppermute(array, axis, [(i, i ^ 1) for i in range(peers)])


def slot_of(ident):
    same = ident[:, None] == ident[None, :]
    count = ident.shape[0]
    order = jnp.arange(count, dtype=jnp.int32)
    before = order[None, :] < order[:, None]
    return jnp.sum((same & before).astype(jnp.int32), axis=1)


def select(rows, width, dtype=jnp.bfloat16):
    return (rows[:, None] == jnp.arange(width, dtype=jnp.int32)[None, :]).astype(dtype)


def on_device(grad_in, expert_ids, gate_weights, back_rows, shared_down):
    hosts = lax.axis_size("expert")
    chips = hosts // CORES
    core = lax.axis_index("expert") % CORES
    other = 1 - core
    buffer_rows, width = back_rows.shape[3:]
    cap = buffer_rows // hosts
    chip_rows = CORES * cap
    part = width // PARTS
    across = [[CORES * z + c for z in range(chips)] for c in range(CORES)]

    def exchanged(pieces):
        return lax.all_to_all(
            pieces, "expert", split_axis=0, concat_axis=0, tiled=True, axis_index_groups=across
        )

    pieces = back_rows[0, 0, 0].reshape(chips, chip_rows * PARTS, part)
    pieces, own_a = lax.optimization_barrier((pieces, grad_in[0, 0]))
    came = exchanged(pieces)
    came = came.reshape(buffer_rows, width)

    from_next = shifted(own_a, "section", -1)
    ident_a = expert_ids[0, 0, :, 0]
    ident_b = expert_ids[1, 0, :, 0]
    own_ident, own_b, from_next = lax.optimization_barrier((ident_a, grad_in[1, 0], from_next))
    from_prev = shifted(own_b, "section", 1)
    ident_mate = swapped(own_ident, "expert")

    scaled = (gate_weights[0][:, None] * from_next.astype(jnp.float32)).astype(jnp.bfloat16)
    scaled_mate = swapped(scaled, "expert")
    chip_tokens = jnp.concatenate([scaled, scaled_mate], axis=0)

    def place(ident, source):
        row = (ident // CORES) * chip_rows + source * cap + slot_of(ident)
        return jnp.where(ident % CORES == core, row, buffer_rows)

    target = jnp.concatenate([place(ident_a, core), place(ident_mate, other)])
    table = (jnp.arange(buffer_rows, dtype=jnp.int32)[:, None] == target[None, :]).astype(jnp.bfloat16)
    packed = jnp.dot(table, chip_tokens, preferred_element_type=jnp.float32).astype(jnp.bfloat16)
    from_prev, came = lax.optimization_barrier((from_prev, came))
    sent = exchanged(packed.reshape(chips, chip_rows * PARTS, part)).reshape(buffer_rows, width)

    lines = jnp.arange(chips * cap, dtype=jnp.int32)
    passed = select((lines // cap) * chip_rows + other * cap + lines % cap, buffer_rows)
    passed = jnp.dot(passed, came, preferred_element_type=jnp.float32).astype(jnp.bfloat16)
    passed = swapped(passed, "expert")
    slot_b = slot_of(ident_b)
    here = ident_b % CORES == core
    from_own = jnp.where(here, (ident_b // CORES) * chip_rows + core * cap + slot_b, buffer_rows)
    from_mate = jnp.where(here, chips * cap, (ident_b // CORES) * cap + slot_b)
    returned = jnp.dot(
        select(from_own, buffer_rows), came, preferred_element_type=jnp.float32
    ) + jnp.dot(select(from_mate, chips * cap), passed, preferred_element_type=jnp.float32)
    section_grad = (from_prev.astype(jnp.float32) + returned).astype(jnp.bfloat16)

    replica = lax.axis_index("dp")
    down_part = shared_down[0]

    def hidden(own):
        mate = swapped(own, "dp")
        first = jnp.where(replica == 0, own, mate)
        second = jnp.where(replica == 0, mate, own)
        tokens = jnp.concatenate([first, second], axis=0)
        return jnp.einsum(
            "td,hd->th", tokens, down_part, preferred_element_type=jnp.float32
        ).astype(jnp.bfloat16)

    next_tokens, _ = lax.optimization_barrier((from_next, packed))
    hidden_grad = jnp.stack([hidden(next_tokens), hidden(from_prev)])
    return (
        sent.reshape(1, 1, 1, buffer_rows, width),
        section_grad[None],
        hidden_grad[:, None],
    )


def solution(mesh):
    placed = (
        P(None, "section", ("expert", "dp"), None),
        P(None, "section", ("expert", "dp"), None),
        P("section", ("expert", "dp")),
        P("section", "dp", "expert", None, None),
        P("section", "dp", None),
    )
    return jax.shard_map(
        on_device,
        mesh=mesh,
        in_specs=placed,
        out_specs=(
            P("section", "dp", "expert", None, None),
            P("section", ("expert", "dp"), None),
            P(None, "section", "expert", "dp"),
        ),
        check_vma=False,
    )
```

```python
import jax
import jax.numpy as jnp
from jax import lax
from jax.sharding import PartitionSpec as P

CORES = 2
PARTS = 4


def shifted(array, axis, by):
    peers = lax.axis_size(axis)
    pairs = [(i, i + by) for i in range(peers) if 0 <= i + by < peers]
    return lax.ppermute(array, axis, pairs)


def swapped(array, axis):
    peers = lax.axis_size(axis)
    return lax.ppermute(array, axis, [(i, i ^ 1) for i in range(peers)])


def slot_of(ident):
    same = ident[:, None] == ident[None, :]
    count = ident.shape[0]
    order = jnp.arange(count, dtype=jnp.int32)
    before = order[None, :] < order[:, None]
    return jnp.sum((same & before).astype(jnp.int32), axis=1)


def select(rows, width, dtype=jnp.bfloat16):
    return (rows[:, None] == jnp.arange(width, dtype=jnp.int32)[None, :]).astype(dtype)


def on_device(grad_in, expert_ids, gate_weights, back_rows, shared_down):
    hosts = lax.axis_size("expert")
    chips = hosts // CORES
    core = lax.axis_index("expert") % CORES
    other = 1 - core
    buffer_rows, width = back_rows.shape[3:]
    cap = buffer_rows // hosts
    chip_rows = CORES * cap
    part = width // PARTS
    across = [[CORES * z + c for z in range(chips)] for c in range(CORES)]

    def exchanged(pieces):
        return lax.all_to_all(
            pieces, "expert", split_axis=0, concat_axis=0, tiled=True, axis_index_groups=across
        )

    pieces = back_rows[0, 0, 0].reshape(chips, chip_rows * PARTS, part)
    pieces, grads = lax.optimization_barrier((pieces, grad_in))
    own_a = grads[0, 0]
    came = exchanged(pieces)
    came = came.reshape(buffer_rows, width)

    from_next = shifted(own_a, "section", -1)
    ident_a = expert_ids[0, 0, :, 0]
    ident_b = expert_ids[1, 0, :, 0]
    own_b, from_next = lax.optimization_barrier((grads[1, 0], from_next))
    from_prev = shifted(own_b, "section", 1)

    tokens = ident_a.shape[0]
    row_a = (ident_a // CORES) * chip_rows + core * cap + slot_of(ident_a)
    here = ident_a % CORES == core
    numbers = jnp.where(here, buffer_rows, row_a).astype(jnp.bfloat16)[None, :]
    numbers = jnp.pad(numbers, ((0, 7), (0, width - tokens)))
    scaled = (gate_weights[0][:, None] * from_next.astype(jnp.float32)).astype(jnp.bfloat16)
    mate = swapped(jnp.concatenate([scaled, numbers], axis=0), "expert")
    target = jnp.concatenate(
        [jnp.where(here, row_a, buffer_rows), mate[tokens, :tokens].astype(jnp.int32)]
    )
    spread = jnp.concatenate(
        [array[:tokens, g * part : (g + 1) * part] for g in range(PARTS) for array in (scaled, mate)],
        axis=0,
    )
    target = jnp.concatenate([target * PARTS + g for g in range(PARTS)])
    line = jnp.arange(buffer_rows * PARTS, dtype=jnp.int32)
    table = (line[:, None] == target[None, :]).astype(jnp.bfloat16)
    packed = jnp.dot(table, spread, preferred_element_type=jnp.float32).astype(jnp.bfloat16)
    packed = packed.reshape(chips, chip_rows * PARTS, part)
    sent = exchanged(packed).reshape(buffer_rows, width)
    from_prev, came = lax.optimization_barrier((from_prev, came))

    lines = jnp.arange(chips * cap, dtype=jnp.int32)
    passed = select((lines // cap) * chip_rows + other * cap + lines % cap, buffer_rows)
    passed = jnp.dot(passed, came, preferred_element_type=jnp.float32).astype(jnp.bfloat16)
    passed = swapped(passed, "expert")
    slot_b = slot_of(ident_b)
    here = ident_b % CORES == core
    from_own = jnp.where(here, (ident_b // CORES) * chip_rows + core * cap + slot_b, buffer_rows)
    from_mate = jnp.where(here, chips * cap, (ident_b // CORES) * cap + slot_b)
    returned = jnp.dot(
        select(from_own, buffer_rows), came, preferred_element_type=jnp.float32
    ) + jnp.dot(select(from_mate, chips * cap), passed, preferred_element_type=jnp.float32)
    section_grad = (from_prev.astype(jnp.float32) + returned).astype(jnp.bfloat16)

    replica = lax.axis_index("dp")
    down_part = shared_down[0]

    def hidden(own):
        mate = swapped(own, "dp")
        first = jnp.where(replica == 0, own, mate)
        second = jnp.where(replica == 0, mate, own)
        tokens = jnp.concatenate([first, second], axis=0)
        return jnp.einsum(
            "td,hd->th", tokens, down_part, preferred_element_type=jnp.float32
        ).astype(jnp.bfloat16)

    next_tokens, _ = lax.optimization_barrier((from_next, packed))
    hidden_grad = jnp.stack([hidden(next_tokens), hidden(from_prev)])
    return (
        sent.reshape(1, 1, 1, buffer_rows, width),
        section_grad[None],
        hidden_grad[:, None],
    )


def solution(mesh):
    placed = (
        P(None, "section", ("expert", "dp"), None),
        P(None, "section", ("expert", "dp"), None),
        P("section", ("expert", "dp")),
        P("section", "dp", "expert", None, None),
        P("section", "dp", None),
    )
    return jax.shard_map(
        on_device,
        mesh=mesh,
        in_specs=placed,
        out_specs=(
            P("section", "dp", "expert", None, None),
            P("section", ("expert", "dp"), None),
            P(None, "section", "expert", "dp"),
        ),
        check_vma=False,
    )
```

```python
import jax
import jax.numpy as jnp
from jax import lax
from jax.experimental import pallas as pl
from jax.experimental.pallas import tpu as pltpu
from jax.sharding import PartitionSpec as P

CORES = 2
PARTS = 4
CHUNK = 32


def shifted(array, axis, by):
    peers = lax.axis_size(axis)
    pairs = [(i, i + by) for i in range(peers) if 0 <= i + by < peers]
    return lax.ppermute(array, axis, pairs)


def swapped(array, axis):
    peers = lax.axis_size(axis)
    return lax.ppermute(array, axis, [(i, i ^ 1) for i in range(peers)])


def slot_of(ident):
    same = ident[:, None] == ident[None, :]
    count = ident.shape[0]
    order = jnp.arange(count, dtype=jnp.int32)
    before = order[None, :] < order[:, None]
    return jnp.sum((same & before).astype(jnp.int32), axis=1)


def select(rows, width, dtype=jnp.bfloat16):
    return (rows[:, None] == jnp.arange(width, dtype=jnp.int32)[None, :]).astype(dtype)


def from_lines(lines):
    total, part = lines.shape
    count, width = total // PARTS, part * PARTS
    chunks, block = count // CHUNK, CHUNK * PARTS

    def kernel(lines_ref, rows_ref, result, out_sem):
        line = lax.broadcasted_iota(jnp.int32, (block, block), 1)
        column = lax.broadcasted_iota(jnp.int32, (block, block), 0)
        table = (column == (line % PARTS) * CHUNK + line // PARTS).astype(jnp.bfloat16)
        leaving = []
        for q in range(chunks):
            moved = jnp.dot(
                table, lines_ref[q * block : (q + 1) * block], preferred_element_type=jnp.float32
            ).astype(jnp.bfloat16)
            for g in range(PARTS):
                result[q, :, g * part : (g + 1) * part] = moved[g * CHUNK : (g + 1) * CHUNK]
            copy = pltpu.make_async_copy(
                result.at[q], rows_ref.at[pl.ds(q * CHUNK, CHUNK)], out_sem.at[q]
            )
            copy.start()
            leaving.append(copy)
        for copy in leaving:
            copy.wait()

    return pl.pallas_call(
        kernel,
        out_shape=jax.ShapeDtypeStruct((count, width), lines.dtype),
        in_specs=[pl.BlockSpec(memory_space=pltpu.VMEM)],
        out_specs=pl.BlockSpec(memory_space=pl.ANY),
        scratch_shapes=[
            pltpu.VMEM((chunks, CHUNK, width), lines.dtype),
            pltpu.SemaphoreType.DMA((chunks,)),
        ],
        compiler_params=pltpu.CompilerParams(vmem_limit_bytes=16 << 20),
        cost_estimate=pl.CostEstimate(
            flops=2 * count * width * block, bytes_accessed=4 * count * width, transcendentals=0
        ),
    )(lines)


def on_device(grad_in, expert_ids, gate_weights, back_rows, shared_down):
    hosts = lax.axis_size("expert")
    chips = hosts // CORES
    core = lax.axis_index("expert") % CORES
    other = 1 - core
    buffer_rows, width = back_rows.shape[3:]
    cap = buffer_rows // hosts
    chip_rows = CORES * cap
    part = width // PARTS
    across = [[CORES * z + c for z in range(chips)] for c in range(CORES)]

    def exchanged(pieces):
        return lax.all_to_all(
            pieces, "expert", split_axis=0, concat_axis=0, tiled=True, axis_index_groups=across
        )

    pieces = back_rows[0, 0, 0].reshape(chips, chip_rows * PARTS, part)
    pieces, grads = lax.optimization_barrier((pieces, grad_in))
    own_a = grads[0, 0]
    came = exchanged(pieces)
    came = came.reshape(buffer_rows, width)

    from_next = shifted(own_a, "section", -1)
    ident_a = expert_ids[0, 0, :, 0]
    ident_b = expert_ids[1, 0, :, 0]
    own_b, from_next = lax.optimization_barrier((grads[1, 0], from_next))
    from_prev = shifted(own_b, "section", 1)

    tokens = ident_a.shape[0]
    row_a = (ident_a // CORES) * chip_rows + core * cap + slot_of(ident_a)
    here = ident_a % CORES == core
    numbers = jnp.where(here, buffer_rows, row_a).astype(jnp.bfloat16)[None, :]
    numbers = jnp.pad(numbers, ((0, 7), (0, width - tokens)))
    scaled = (gate_weights[0][:, None] * from_next.astype(jnp.float32)).astype(jnp.bfloat16)
    mate = swapped(jnp.concatenate([scaled, numbers], axis=0), "expert")
    target = jnp.concatenate(
        [jnp.where(here, row_a, buffer_rows), mate[tokens, :tokens].astype(jnp.int32)]
    )
    spread = jnp.concatenate(
        [array[:tokens, g * part : (g + 1) * part] for g in range(PARTS) for array in (scaled, mate)],
        axis=0,
    )
    target = jnp.concatenate([target * PARTS + g for g in range(PARTS)])
    line = jnp.arange(buffer_rows * PARTS, dtype=jnp.int32)
    table = (line[:, None] == target[None, :]).astype(jnp.bfloat16)
    packed = jnp.dot(table, spread, preferred_element_type=jnp.float32).astype(jnp.bfloat16)
    packed = packed.reshape(chips, chip_rows * PARTS, part)
    sent = from_lines(exchanged(packed).reshape(buffer_rows * PARTS, part))
    from_prev, came = lax.optimization_barrier((from_prev, came))

    lines = jnp.arange(chips * cap, dtype=jnp.int32)
    passed = select((lines // cap) * chip_rows + other * cap + lines % cap, buffer_rows)
    passed = jnp.dot(passed, came, preferred_element_type=jnp.float32).astype(jnp.bfloat16)
    passed = swapped(passed, "expert")
    slot_b = slot_of(ident_b)
    here = ident_b % CORES == core
    from_own = jnp.where(here, (ident_b // CORES) * chip_rows + core * cap + slot_b, buffer_rows)
    from_mate = jnp.where(here, chips * cap, (ident_b // CORES) * cap + slot_b)
    returned = jnp.dot(
        select(from_own, buffer_rows), came, preferred_element_type=jnp.float32
    ) + jnp.dot(select(from_mate, chips * cap), passed, preferred_element_type=jnp.float32)
    section_grad = (from_prev.astype(jnp.float32) + returned).astype(jnp.bfloat16)

    replica = lax.axis_index("dp")
    down_part = shared_down[0]

    def hidden(own):
        mate = swapped(own, "dp")
        first = jnp.where(replica == 0, own, mate)
        second = jnp.where(replica == 0, mate, own)
        tokens = jnp.concatenate([first, second], axis=0)
        return jnp.einsum(
            "td,hd->th", tokens, down_part, preferred_element_type=jnp.float32
        ).astype(jnp.bfloat16)

    next_tokens, _ = lax.optimization_barrier((from_next, packed))
    hidden_grad = jnp.stack([hidden(next_tokens), hidden(from_prev)])
    return (
        sent.reshape(1, 1, 1, buffer_rows, width),
        section_grad[None],
        hidden_grad[:, None],
    )


def solution(mesh):
    placed = (
        P(None, "section", ("expert", "dp"), None),
        P(None, "section", ("expert", "dp"), None),
        P("section", ("expert", "dp")),
        P("section", "dp", "expert", None, None),
        P("section", "dp", None),
    )
    return jax.shard_map(
        on_device,
        mesh=mesh,
        in_specs=placed,
        out_specs=(
            P("section", "dp", "expert", None, None),
            P("section", ("expert", "dp"), None),
            P(None, "section", "expert", "dp"),
        ),
        check_vma=False,
    )
```

```python
import jax
import jax.numpy as jnp
from jax import lax
from jax.experimental import pallas as pl
from jax.experimental.pallas import tpu as pltpu
from jax.sharding import PartitionSpec as P

CORES = 2
PARTS = 4
CHUNK = 32


def shifted(array, axis, by):
    peers = lax.axis_size(axis)
    pairs = [(i, i + by) for i in range(peers) if 0 <= i + by < peers]
    return lax.ppermute(array, axis, pairs)


def swapped(array, axis):
    peers = lax.axis_size(axis)
    return lax.ppermute(array, axis, [(i, i ^ 1) for i in range(peers)])


def slot_of(ident):
    same = ident[:, None] == ident[None, :]
    count = ident.shape[0]
    order = jnp.arange(count, dtype=jnp.int32)
    before = order[None, :] < order[:, None]
    return jnp.sum((same & before).astype(jnp.int32), axis=1)


def select(rows, width, dtype=jnp.bfloat16):
    return (rows[:, None] == jnp.arange(width, dtype=jnp.int32)[None, :]).astype(dtype)


def from_lines(lines):
    total, part = lines.shape
    count, width = total // PARTS, part * PARTS
    chunks, block = count // CHUNK, CHUNK * PARTS

    def kernel(lines_ref, rows_ref, result, out_sem):
        line = lax.broadcasted_iota(jnp.int32, (block, block), 1)
        column = lax.broadcasted_iota(jnp.int32, (block, block), 0)
        table = (column == (line % PARTS) * CHUNK + line // PARTS).astype(jnp.bfloat16)
        leaving = []
        for q in range(chunks):
            moved = jnp.dot(
                table, lines_ref[q * block : (q + 1) * block], preferred_element_type=jnp.float32
            ).astype(jnp.bfloat16)
            for g in range(PARTS):
                result[q, :, g * part : (g + 1) * part] = moved[g * CHUNK : (g + 1) * CHUNK]
            copy = pltpu.make_async_copy(
                result.at[q], rows_ref.at[pl.ds(q * CHUNK, CHUNK)], out_sem.at[q]
            )
            copy.start()
            leaving.append(copy)
        for copy in leaving:
            copy.wait()

    return pl.pallas_call(
        kernel,
        out_shape=jax.ShapeDtypeStruct((count, width), lines.dtype),
        in_specs=[pl.BlockSpec(memory_space=pltpu.VMEM)],
        out_specs=pl.BlockSpec(memory_space=pl.ANY),
        scratch_shapes=[
            pltpu.VMEM((chunks, CHUNK, width), lines.dtype),
            pltpu.SemaphoreType.DMA((chunks,)),
        ],
        compiler_params=pltpu.CompilerParams(vmem_limit_bytes=16 << 20),
        cost_estimate=pl.CostEstimate(
            flops=2 * count * width * block, bytes_accessed=4 * count * width, transcendentals=0
        ),
    )(lines)


def on_device(grad_in, expert_ids, gate_weights, back_rows, shared_down):
    hosts = lax.axis_size("expert")
    chips = hosts // CORES
    core = lax.axis_index("expert") % CORES
    other = 1 - core
    buffer_rows, width = back_rows.shape[3:]
    cap = buffer_rows // hosts
    chip_rows = CORES * cap
    part = width // PARTS
    across = [[CORES * z + c for z in range(chips)] for c in range(CORES)]

    def exchanged(pieces):
        return lax.all_to_all(
            pieces, "expert", split_axis=0, concat_axis=0, tiled=True, axis_index_groups=across
        )

    total = buffer_rows * PARTS
    order = jnp.arange(total, dtype=jnp.int32)
    order = (order % PARTS) * buffer_rows + order // PARTS
    back = back_rows[0, 0, 0]
    back = jnp.concatenate([back[:, g * part : (g + 1) * part] for g in range(PARTS)], axis=0)
    pieces = jnp.dot(select(order, total), back, preferred_element_type=jnp.float32)
    pieces = pieces.astype(jnp.bfloat16).reshape(chips, chip_rows * PARTS, part)
    pieces, grads = lax.optimization_barrier((pieces, grad_in))
    own_a = grads[0, 0]
    came = exchanged(pieces)
    came = came.reshape(buffer_rows, width)

    from_next = shifted(own_a, "section", -1)
    ident_a = expert_ids[0, 0, :, 0]
    ident_b = expert_ids[1, 0, :, 0]
    own_b, from_next = lax.optimization_barrier((grads[1, 0], from_next))
    from_prev = shifted(own_b, "section", 1)

    tokens = ident_a.shape[0]
    row_a = (ident_a // CORES) * chip_rows + core * cap + slot_of(ident_a)
    here = ident_a % CORES == core
    numbers = jnp.where(here, buffer_rows, row_a).astype(jnp.bfloat16)[None, :]
    numbers = jnp.pad(numbers, ((0, 7), (0, width - tokens)))
    scaled = (gate_weights[0][:, None] * from_next.astype(jnp.float32)).astype(jnp.bfloat16)
    mate = swapped(jnp.concatenate([scaled, numbers], axis=0), "expert")
    target = jnp.concatenate(
        [jnp.where(here, row_a, buffer_rows), mate[tokens, :tokens].astype(jnp.int32)]
    )
    spread = jnp.concatenate(
        [array[:tokens, g * part : (g + 1) * part] for g in range(PARTS) for array in (scaled, mate)],
        axis=0,
    )
    target = jnp.concatenate([target * PARTS + g for g in range(PARTS)])
    line = jnp.arange(buffer_rows * PARTS, dtype=jnp.int32)
    table = (line[:, None] == target[None, :]).astype(jnp.bfloat16)
    packed = jnp.dot(table, spread, preferred_element_type=jnp.float32).astype(jnp.bfloat16)
    packed = packed.reshape(chips, chip_rows * PARTS, part)
    sent = from_lines(exchanged(packed).reshape(buffer_rows * PARTS, part))
    from_prev, came = lax.optimization_barrier((from_prev, came))

    lines = jnp.arange(chips * cap, dtype=jnp.int32)
    passed = select((lines // cap) * chip_rows + other * cap + lines % cap, buffer_rows)
    passed = jnp.dot(passed, came, preferred_element_type=jnp.float32).astype(jnp.bfloat16)
    passed = swapped(passed, "expert")
    slot_b = slot_of(ident_b)
    here = ident_b % CORES == core
    from_own = jnp.where(here, (ident_b // CORES) * chip_rows + core * cap + slot_b, buffer_rows)
    from_mate = jnp.where(here, chips * cap, (ident_b // CORES) * cap + slot_b)
    returned = jnp.dot(
        select(from_own, buffer_rows), came, preferred_element_type=jnp.float32
    ) + jnp.dot(select(from_mate, chips * cap), passed, preferred_element_type=jnp.float32)
    section_grad = (from_prev.astype(jnp.float32) + returned).astype(jnp.bfloat16)

    replica = lax.axis_index("dp")
    down_part = shared_down[0]

    def hidden(own):
        mate = swapped(own, "dp")
        first = jnp.where(replica == 0, own, mate)
        second = jnp.where(replica == 0, mate, own)
        tokens = jnp.concatenate([first, second], axis=0)
        return jnp.einsum(
            "td,hd->th", tokens, down_part, preferred_element_type=jnp.float32
        ).astype(jnp.bfloat16)

    next_tokens, _ = lax.optimization_barrier((from_next, packed))
    hidden_grad = jnp.stack([hidden(next_tokens), hidden(from_prev)])
    return (
        sent.reshape(1, 1, 1, buffer_rows, width),
        section_grad[None],
        hidden_grad[:, None],
    )


def solution(mesh):
    placed = (
        P(None, "section", ("expert", "dp"), None),
        P(None, "section", ("expert", "dp"), None),
        P("section", ("expert", "dp")),
        P("section", "dp", "expert", None, None),
        P("section", "dp", None),
    )
    return jax.shard_map(
        on_device,
        mesh=mesh,
        in_specs=placed,
        out_specs=(
            P("section", "dp", "expert", None, None),
            P("section", ("expert", "dp"), None),
            P(None, "section", "expert", "dp"),
        ),
        check_vma=False,
    )
```

```python
import jax
import jax.numpy as jnp
from jax import lax
from jax.experimental import pallas as pl
from jax.experimental.pallas import tpu as pltpu
from jax.sharding import PartitionSpec as P

CORES = 2
PARTS = 4
CHUNK = 32


def shifted(array, axis, by):
    peers = lax.axis_size(axis)
    pairs = [(i, i + by) for i in range(peers) if 0 <= i + by < peers]
    return lax.ppermute(array, axis, pairs)


def swapped(array, axis):
    peers = lax.axis_size(axis)
    return lax.ppermute(array, axis, [(i, i ^ 1) for i in range(peers)])


def slot_of(ident):
    same = ident[:, None] == ident[None, :]
    count = ident.shape[0]
    order = jnp.arange(count, dtype=jnp.int32)
    before = order[None, :] < order[:, None]
    return jnp.sum((same & before).astype(jnp.int32), axis=1)


def select(rows, width, dtype=jnp.bfloat16):
    return (rows[:, None] == jnp.arange(width, dtype=jnp.int32)[None, :]).astype(dtype)


def into_lines(rows):
    count, width = rows.shape
    part = width // PARTS
    chunks, block = count // CHUNK, CHUNK * PARTS

    def kernel(rows_ref, lines_ref, held, result, in_sem, out_sem):
        arriving = [
            pltpu.make_async_copy(rows_ref.at[pl.ds(q * CHUNK, CHUNK)], held.at[q], in_sem.at[q])
            for q in range(chunks)
        ]
        for copy in arriving:
            copy.start()
        line = lax.broadcasted_iota(jnp.int32, (block, block), 0)
        column = lax.broadcasted_iota(jnp.int32, (block, block), 1)
        table = (column == (line % PARTS) * CHUNK + line // PARTS).astype(jnp.bfloat16)
        leaving = []
        for q in range(chunks):
            arriving[q].wait()
            stacked = jnp.concatenate(
                [held[q, :, g * part : (g + 1) * part] for g in range(PARTS)], axis=0
            )
            moved = jnp.dot(table, stacked, preferred_element_type=jnp.float32)
            result[q] = moved.astype(jnp.bfloat16)
            copy = pltpu.make_async_copy(
                result.at[q], lines_ref.at[pl.ds(q * block, block)], out_sem.at[q]
            )
            copy.start()
            leaving.append(copy)
        for copy in leaving:
            copy.wait()

    return pl.pallas_call(
        kernel,
        out_shape=jax.ShapeDtypeStruct((count * PARTS, part), rows.dtype),
        in_specs=[pl.BlockSpec(memory_space=pl.ANY)],
        out_specs=pl.BlockSpec(memory_space=pl.ANY),
        scratch_shapes=[
            pltpu.VMEM((chunks, CHUNK, width), rows.dtype),
            pltpu.VMEM((chunks, block, part), rows.dtype),
            pltpu.SemaphoreType.DMA((chunks,)),
            pltpu.SemaphoreType.DMA((chunks,)),
        ],
        compiler_params=pltpu.CompilerParams(vmem_limit_bytes=60 << 20),
        cost_estimate=pl.CostEstimate(
            flops=2 * count * width * block, bytes_accessed=4 * count * width, transcendentals=0
        ),
    )(rows)


def from_lines(lines):
    total, part = lines.shape
    count, width = total // PARTS, part * PARTS
    chunks, block = count // CHUNK, CHUNK * PARTS

    def kernel(lines_ref, rows_ref, result, out_sem):
        line = lax.broadcasted_iota(jnp.int32, (block, block), 1)
        column = lax.broadcasted_iota(jnp.int32, (block, block), 0)
        table = (column == (line % PARTS) * CHUNK + line // PARTS).astype(jnp.bfloat16)
        leaving = []
        for q in range(chunks):
            moved = jnp.dot(
                table, lines_ref[q * block : (q + 1) * block], preferred_element_type=jnp.float32
            ).astype(jnp.bfloat16)
            for g in range(PARTS):
                result[q, :, g * part : (g + 1) * part] = moved[g * CHUNK : (g + 1) * CHUNK]
            copy = pltpu.make_async_copy(
                result.at[q], rows_ref.at[pl.ds(q * CHUNK, CHUNK)], out_sem.at[q]
            )
            copy.start()
            leaving.append(copy)
        for copy in leaving:
            copy.wait()

    return pl.pallas_call(
        kernel,
        out_shape=jax.ShapeDtypeStruct((count, width), lines.dtype),
        in_specs=[pl.BlockSpec(memory_space=pltpu.VMEM)],
        out_specs=pl.BlockSpec(memory_space=pl.ANY),
        scratch_shapes=[
            pltpu.VMEM((chunks, CHUNK, width), lines.dtype),
            pltpu.SemaphoreType.DMA((chunks,)),
        ],
        compiler_params=pltpu.CompilerParams(vmem_limit_bytes=16 << 20),
        cost_estimate=pl.CostEstimate(
            flops=2 * count * width * block, bytes_accessed=4 * count * width, transcendentals=0
        ),
    )(lines)


def on_device(grad_in, expert_ids, gate_weights, back_rows, shared_down):
    hosts = lax.axis_size("expert")
    chips = hosts // CORES
    core = lax.axis_index("expert") % CORES
    other = 1 - core
    buffer_rows, width = back_rows.shape[3:]
    cap = buffer_rows // hosts
    chip_rows = CORES * cap
    part = width // PARTS
    across = [[CORES * z + c for z in range(chips)] for c in range(CORES)]

    def exchanged(pieces):
        return lax.all_to_all(
            pieces, "expert", split_axis=0, concat_axis=0, tiled=True, axis_index_groups=across
        )

    pieces = into_lines(back_rows[0, 0, 0]).reshape(chips, chip_rows * PARTS, part)
    pieces, grads = lax.optimization_barrier((pieces, grad_in))
    own_a = grads[0, 0]
    came = exchanged(pieces)
    came = came.reshape(buffer_rows, width)

    from_next = shifted(own_a, "section", -1)
    ident_a = expert_ids[0, 0, :, 0]
    ident_b = expert_ids[1, 0, :, 0]
    own_b, from_next = lax.optimization_barrier((grads[1, 0], from_next))
    from_prev = shifted(own_b, "section", 1)

    tokens = ident_a.shape[0]
    row_a = (ident_a // CORES) * chip_rows + core * cap + slot_of(ident_a)
    here = ident_a % CORES == core
    numbers = jnp.where(here, buffer_rows, row_a).astype(jnp.bfloat16)[None, :]
    numbers = jnp.pad(numbers, ((0, 7), (0, width - tokens)))
    scaled = (gate_weights[0][:, None] * from_next.astype(jnp.float32)).astype(jnp.bfloat16)
    mate = swapped(jnp.concatenate([scaled, numbers], axis=0), "expert")
    target = jnp.concatenate(
        [jnp.where(here, row_a, buffer_rows), mate[tokens, :tokens].astype(jnp.int32)]
    )
    spread = jnp.concatenate(
        [array[:tokens, g * part : (g + 1) * part] for g in range(PARTS) for array in (scaled, mate)],
        axis=0,
    )
    target = jnp.concatenate([target * PARTS + g for g in range(PARTS)])
    line = jnp.arange(buffer_rows * PARTS, dtype=jnp.int32)
    table = (line[:, None] == target[None, :]).astype(jnp.bfloat16)
    packed = jnp.dot(table, spread, preferred_element_type=jnp.float32).astype(jnp.bfloat16)
    packed = packed.reshape(chips, chip_rows * PARTS, part)
    sent = from_lines(exchanged(packed).reshape(buffer_rows * PARTS, part))
    from_prev, came = lax.optimization_barrier((from_prev, came))

    lines = jnp.arange(chips * cap, dtype=jnp.int32)
    passed = select((lines // cap) * chip_rows + other * cap + lines % cap, buffer_rows)
    passed = jnp.dot(passed, came, preferred_element_type=jnp.float32).astype(jnp.bfloat16)
    passed = swapped(passed, "expert")
    slot_b = slot_of(ident_b)
    here = ident_b % CORES == core
    from_own = jnp.where(here, (ident_b // CORES) * chip_rows + core * cap + slot_b, buffer_rows)
    from_mate = jnp.where(here, chips * cap, (ident_b // CORES) * cap + slot_b)
    returned = jnp.dot(
        select(from_own, buffer_rows), came, preferred_element_type=jnp.float32
    ) + jnp.dot(select(from_mate, chips * cap), passed, preferred_element_type=jnp.float32)
    section_grad = (from_prev.astype(jnp.float32) + returned).astype(jnp.bfloat16)

    replica = lax.axis_index("dp")
    down_part = shared_down[0]

    def hidden(own):
        mate = swapped(own, "dp")
        first = jnp.where(replica == 0, own, mate)
        second = jnp.where(replica == 0, mate, own)
        tokens = jnp.concatenate([first, second], axis=0)
        return jnp.einsum(
            "td,hd->th", tokens, down_part, preferred_element_type=jnp.float32
        ).astype(jnp.bfloat16)

    next_tokens, _ = lax.optimization_barrier((from_next, packed))
    hidden_grad = jnp.stack([hidden(next_tokens), hidden(from_prev)])
    return (
        sent.reshape(1, 1, 1, buffer_rows, width),
        section_grad[None],
        hidden_grad[:, None],
    )


def solution(mesh):
    placed = (
        P(None, "section", ("expert", "dp"), None),
        P(None, "section", ("expert", "dp"), None),
        P("section", ("expert", "dp")),
        P("section", "dp", "expert", None, None),
        P("section", "dp", None),
    )
    return jax.shard_map(
        on_device,
        mesh=mesh,
        in_specs=placed,
        out_specs=(
            P("section", "dp", "expert", None, None),
            P("section", ("expert", "dp"), None),
            P(None, "section", "expert", "dp"),
        ),
        check_vma=False,
    )
```

```python
import jax
import jax.numpy as jnp
from jax import lax
from jax.experimental import pallas as pl
from jax.experimental.pallas import tpu as pltpu
from jax.sharding import PartitionSpec as P

CORES = 2
PARTS = 4
CHUNK = 48


def shifted(array, axis, by):
    peers = lax.axis_size(axis)
    pairs = [(i, i + by) for i in range(peers) if 0 <= i + by < peers]
    return lax.ppermute(array, axis, pairs)


def swapped(array, axis):
    peers = lax.axis_size(axis)
    return lax.ppermute(array, axis, [(i, i ^ 1) for i in range(peers)])


def slot_of(ident):
    same = ident[:, None] == ident[None, :]
    count = ident.shape[0]
    order = jnp.arange(count, dtype=jnp.int32)
    before = order[None, :] < order[:, None]
    return jnp.sum((same & before).astype(jnp.int32), axis=1)


def select(rows, width, dtype=jnp.bfloat16):
    return (rows[:, None] == jnp.arange(width, dtype=jnp.int32)[None, :]).astype(dtype)


def from_lines(lines):
    total, part = lines.shape
    count, width = total // PARTS, part * PARTS
    chunks, block = count // CHUNK, CHUNK * PARTS

    def kernel(lines_ref, rows_ref, result, out_sem):
        line = lax.broadcasted_iota(jnp.int32, (block, block), 1)
        column = lax.broadcasted_iota(jnp.int32, (block, block), 0)
        table = (column == (line % PARTS) * CHUNK + line // PARTS).astype(jnp.bfloat16)
        leaving = []
        for q in range(chunks):
            moved = jnp.dot(
                table, lines_ref[q * block : (q + 1) * block], preferred_element_type=jnp.float32
            ).astype(jnp.bfloat16)
            for g in range(PARTS):
                result[q, :, g * part : (g + 1) * part] = moved[g * CHUNK : (g + 1) * CHUNK]
            copy = pltpu.make_async_copy(
                result.at[q], rows_ref.at[pl.ds(q * CHUNK, CHUNK)], out_sem.at[q]
            )
            copy.start()
            leaving.append(copy)
        for copy in leaving:
            copy.wait()

    return pl.pallas_call(
        kernel,
        out_shape=jax.ShapeDtypeStruct((count, width), lines.dtype),
        in_specs=[pl.BlockSpec(memory_space=pltpu.VMEM)],
        out_specs=pl.BlockSpec(memory_space=pl.ANY),
        scratch_shapes=[
            pltpu.VMEM((chunks, CHUNK, width), lines.dtype),
            pltpu.SemaphoreType.DMA((chunks,)),
        ],
        compiler_params=pltpu.CompilerParams(vmem_limit_bytes=16 << 20),
        cost_estimate=pl.CostEstimate(
            flops=2 * count * width * block, bytes_accessed=4 * count * width, transcendentals=0
        ),
    )(lines)


def on_device(grad_in, expert_ids, gate_weights, back_rows, shared_down):
    hosts = lax.axis_size("expert")
    chips = hosts // CORES
    core = lax.axis_index("expert") % CORES
    other = 1 - core
    buffer_rows, width = back_rows.shape[3:]
    cap = buffer_rows // hosts
    chip_rows = CORES * cap
    part = width // PARTS
    across = [[CORES * z + c for z in range(chips)] for c in range(CORES)]

    def exchanged(pieces):
        return lax.all_to_all(
            pieces, "expert", split_axis=0, concat_axis=0, tiled=True, axis_index_groups=across
        )

    pieces = back_rows[0, 0, 0].reshape(chips, chip_rows * PARTS, part)
    pieces, grads = lax.optimization_barrier((pieces, grad_in))
    own_a = grads[0, 0]
    came = exchanged(pieces)
    came = came.reshape(buffer_rows, width)

    from_next = shifted(own_a, "section", -1)
    ident_a = expert_ids[0, 0, :, 0]
    ident_b = expert_ids[1, 0, :, 0]
    own_b, from_next = lax.optimization_barrier((grads[1, 0], from_next))
    from_prev = shifted(own_b, "section", 1)

    tokens = ident_a.shape[0]
    row_a = (ident_a // CORES) * chip_rows + core * cap + slot_of(ident_a)
    here = ident_a % CORES == core
    numbers = jnp.where(here, buffer_rows, row_a).astype(jnp.bfloat16)[None, :]
    numbers = jnp.pad(numbers, ((0, 7), (0, width - tokens)))
    scaled = (gate_weights[0][:, None] * from_next.astype(jnp.float32)).astype(jnp.bfloat16)
    mate = swapped(jnp.concatenate([scaled, numbers], axis=0), "expert")
    target = jnp.concatenate(
        [jnp.where(here, row_a, buffer_rows), mate[tokens, :tokens].astype(jnp.int32)]
    )
    spread = jnp.concatenate(
        [array[:tokens, g * part : (g + 1) * part] for g in range(PARTS) for array in (scaled, mate)],
        axis=0,
    )
    target = jnp.concatenate([target * PARTS + g for g in range(PARTS)])
    line = jnp.arange(buffer_rows * PARTS, dtype=jnp.int32)
    table = (line[:, None] == target[None, :]).astype(jnp.bfloat16)
    packed = jnp.dot(table, spread, preferred_element_type=jnp.float32).astype(jnp.bfloat16)
    packed = packed.reshape(chips, chip_rows * PARTS, part)
    sent = from_lines(exchanged(packed).reshape(buffer_rows * PARTS, part))
    from_prev, came = lax.optimization_barrier((from_prev, came))

    lines = jnp.arange(chips * cap, dtype=jnp.int32)
    passed = select((lines // cap) * chip_rows + other * cap + lines % cap, buffer_rows)
    passed = jnp.dot(passed, came, preferred_element_type=jnp.float32).astype(jnp.bfloat16)
    passed = swapped(passed, "expert")
    slot_b = slot_of(ident_b)
    here = ident_b % CORES == core
    from_own = jnp.where(here, (ident_b // CORES) * chip_rows + core * cap + slot_b, buffer_rows)
    from_mate = jnp.where(here, chips * cap, (ident_b // CORES) * cap + slot_b)
    returned = jnp.dot(
        select(from_own, buffer_rows), came, preferred_element_type=jnp.float32
    ) + jnp.dot(select(from_mate, chips * cap), passed, preferred_element_type=jnp.float32)
    section_grad = (from_prev.astype(jnp.float32) + returned).astype(jnp.bfloat16)

    replica = lax.axis_index("dp")
    down_part = shared_down[0]

    def hidden(own):
        mate = swapped(own, "dp")
        first = jnp.where(replica == 0, own, mate)
        second = jnp.where(replica == 0, mate, own)
        tokens = jnp.concatenate([first, second], axis=0)
        return jnp.einsum(
            "td,hd->th", tokens, down_part, preferred_element_type=jnp.float32
        ).astype(jnp.bfloat16)

    next_tokens, _ = lax.optimization_barrier((from_next, packed))
    hidden_grad = jnp.stack([hidden(next_tokens), hidden(from_prev)])
    return (
        sent.reshape(1, 1, 1, buffer_rows, width),
        section_grad[None],
        hidden_grad[:, None],
    )


def solution(mesh):
    placed = (
        P(None, "section", ("expert", "dp"), None),
        P(None, "section", ("expert", "dp"), None),
        P("section", ("expert", "dp")),
        P("section", "dp", "expert", None, None),
        P("section", "dp", None),
    )
    return jax.shard_map(
        on_device,
        mesh=mesh,
        in_specs=placed,
        out_specs=(
            P("section", "dp", "expert", None, None),
            P("section", ("expert", "dp"), None),
            P(None, "section", "expert", "dp"),
        ),
        check_vma=False,
    )
```
